32 devices in a mesh: gx: 8 (over y, x, core), gy: 4 (over z).
Axes of the slice: x: 2, y: 2, z: 4, core: 2. Of those that a mesh axis runs over, the one named last changes fastest.
Arguments:
- populations: float32 [19, 8, 256, 512], P(None, None, 'gx', 'gy'), may hold values from 0.6 to 1.4
- concentrations: float32 [2, 8, 256, 512], P(None, None, 'gx', 'gy'), may hold values from 0.3 to 3
- potential: float32 [8, 256, 512], P(None, 'gx', 'gy'), may hold values from -4 to 4
- permittivity: float32 [8, 256, 512], P(None, 'gx', 'gy'), may hold values from 0.3 to 3
- solid: int32 [8, 256, 512], P(None, 'gx', 'gy'), may hold values 0 or 1
- bead_label: int32 [8, 256, 512], P(None, 'gx', 'gy'), may hold values from 0 to 4, as said below
- bead_charge: float32 [4], replicated, may hold values from -2 to 1
- rates: float32 [5], replicated, may hold values from 0.7 to 1.9
- diffusivity: float32 [2], replicated, may hold values from 0.03 to 0.12
Outputs:
- populations_out: float32 [19, 8, 256, 512], P(None, None, 'gx', 'gy')
- concentrations_out: float32 [2, 8, 256, 512], P(None, None, 'gx', 'gy')
- potential_out: float32 [8, 256, 512], P(None, 'gx', 'gy')
The draws below stay inside these ranges and needn't reach their ends.
Inputs may be any that keep to these rules, and one draw needn't show every extreme that they name: `solid`: 1 marks a pore-wall cell. `bead_label`: 0 marks a cell without a bead; 1 to 4 select an entry of bead_charge.
All inputs are finite; a program needn't handle non-finite values. No bound on the sum of `solid` on one device may be relied on, other than what follows from the above.
Results may differ from the reference program's by a relative error of at most 0.0001.
Values sent between devices are 32-bit elements; how exact they have to be, the bound alone decides.
A program may use at most 64 MiB of HBM per device.

```python
import math
import jax
import jax.numpy as jnp
import numpy as np
from jax import lax

NZ = 8
STEPS = 8
SWEEPS = 3
NX = 256
NY = 512


def draw_bead_label(key, part):
    key_one, key_two = jax.random.split(jax.random.fold_in(key, 17))
    labels_all = jax.random.randint(key_one, (NZ, NX, NY), 1, 5)
    placed_mask = jax.random.randint(key_two, (NZ, NX, NY), 0, 4)
    return jnp.where(placed_mask == 0, labels_all, 0).astype(jnp.int32)


def place_ends(entries, own_key, least, top_value):
    longest = entries.shape.index(max(entries.shape))
    spots = []
    for shift in (0, 1):
        where = [jax.random.randint(jax.random.fold_in(own_key, axis), (), 0, length) for axis, length in enumerate(entries.shape)]
        where[longest] = (where[longest] + shift) % entries.shape[longest]
        spots.append(tuple(where))
    return entries.at[spots[0]].set(least).at[spots[1]].set(top_value)


def block_scale(key, dims, pieces, least, largest):
    loudness, own = 1.0, jax.random.fold_in(key, 6)
    for axis_at, shards_of in pieces:
        steps = jnp.exp(jax.random.uniform(jax.random.fold_in(own, axis_at), (shards_of,), jnp.float32, least / len(pieces), largest / len(pieces)))
        loudness = loudness * jnp.repeat(steps, dims[axis_at] // shards_of).reshape([-1 if axis == axis_at else 1 for axis in range(len(dims))])
    return loudness


def noise(key, shape, scale, limit, shards=(), kind=jnp.bfloat16):
    entries = jax.random.normal(key, shape, jnp.float32) * scale
    if len(shards) > 0:
        entries = block_scale(key, shape, shards, -0.22, 0.18) * entries
    return jnp.clip(entries, min=-limit, max=limit).astype(kind)


def setup_inputs(seed: int = 0) -> dict:
    splits = jax.random.split(jax.random.key(seed), 10)
    populations = jnp.clip(0.6 + 0.79999995 * jax.random.uniform(splits[0], (19, NZ, NX, NY), jnp.float32) ** block_scale(splits[0], (19, NZ, NX, NY), ((2, 8), (3, 4)), -0.2, 0.2), 0.6, 1.4)
    concentrations = jnp.clip(jnp.exp(math.log(3.0) - 2.3025851 * jax.random.uniform(splits[1], (2, NZ, NX, NY), jnp.float32) ** block_scale(splits[1], (2, NZ, NX, NY), ((2, 8), (3, 4)), -0.2, 0.2)), 0.3, 3.0)
    potential = noise(splits[2], (NZ, NX, NY), 1.0, 4.0, ((1, 8), (2, 4)), jnp.float32)
    permittivity = jnp.clip(jnp.exp(math.log(3.0) - 2.3025851 * jax.random.uniform(splits[3], (NZ, NX, NY), jnp.float32) ** block_scale(splits[3], (NZ, NX, NY), ((1, 8), (2, 4)), -0.2, 0.2)), 0.3, 3.0)
    solid = place_ends((jax.random.randint(splits[4], (NZ, NX, NY), 0, 6) < 1).astype(jnp.int32), jax.random.fold_in(splits[4], 1), 0, 1)
    bead_label = draw_bead_label(jax.random.fold_in(splits[9], 71), 0)
    bead_charge = jnp.clip(jax.random.uniform(splits[6], (4,), jnp.float32, -2.0, 1.0), -2.0, 1.0)
    rates = jnp.clip(jnp.exp(jax.random.uniform(splits[7], (5,), jnp.float32, math.log(0.7), math.log(1.9))), 0.7, 1.9)
    diffusivity = jnp.clip(jnp.exp(jax.random.uniform(splits[8], (2,), jnp.float32, math.log(0.03), math.log(0.12))), 0.03, 0.12)
    return {"populations": populations, "concentrations": concentrations, "potential": potential, "permittivity": permittivity, "solid": solid, "bead_label": bead_label, "bead_charge": bead_charge, "rates": rates, "diffusivity": diffusivity}


VELOCITIES = np.array([[0, 0, 0], [1, 0, 0], [-1, 0, 0], [0, 1, 0], [0, -1, 0], [0, 0, 1], [0, 0, -1],
                       [1, 1, 0], [-1, -1, 0], [1, -1, 0], [-1, 1, 0], [1, 0, 1], [-1, 0, -1], [1, 0, -1],
                       [-1, 0, 1], [0, 1, 1], [0, -1, -1], [0, 1, -1], [0, -1, 1]])
RATE_SLOTS = np.array([5, 0, 1, 5, 2, 5, 2, 5, 2, 3, 1, 3, 1, 3, 3, 3, 4, 4, 4])
FORCE_SCALE = 0.02
EXT_FIELD = 0.05
HIGHEST = lax.Precision.HIGHEST


def lattice_weights():
    square = np.sum(VELOCITIES * VELOCITIES, axis=1)
    return np.where(square == 0, 1.0 / 3.0, np.where(square == 1, 1.0 / 18.0, 1.0 / 36.0))


def opposites():
    return [int(np.argmax(np.all(VELOCITIES == -VELOCITIES[member], axis=1))) for member in range(19)]


def moment_matrix():
    veloc = VELOCITIES * 1.0
    along_x, along_y, along_z = veloc[:, 0], veloc[:, 1], veloc[:, 2]
    square = along_x * along_x + along_y * along_y + along_z * along_z
    heat = 5.0 * square - 9.0
    ghost = 3.0 * square - 5.0
    normal_xx = 3.0 * along_x * along_x - square
    normal_ww = along_y * along_y - along_z * along_z
    rows = [np.ones(19), 19.0 * square - 30.0, (21.0 * square * square - 53.0 * square + 24.0) / 2.0,
            along_x, heat * along_x, along_y, heat * along_y, along_z, heat * along_z,
            normal_xx, ghost * normal_xx, normal_ww, ghost * normal_ww,
            along_x * along_y, along_y * along_z, along_x * along_z,
            (along_y * along_y - along_z * along_z) * along_x,
            (along_z * along_z - along_x * along_x) * along_y,
            (along_x * along_x - along_y * along_y) * along_z]
    return np.stack(rows)


def relaxation(rates):
    weights = lattice_weights()
    matrix = moment_matrix()
    norms = np.sum(matrix * matrix, axis=1)
    left_side = (matrix.T / norms[None, :]) / weights[:, None]
    right_side = matrix * weights[None, :]
    full = jnp.concatenate([rates, jnp.ones((1,), jnp.float32)])
    strength = full[jnp.asarray(RATE_SLOTS)]
    return jnp.dot(jnp.asarray(left_side, jnp.float32) * strength[None, :], jnp.asarray(right_side, jnp.float32), precision=HIGHEST)


def bead_density(bead_label, bead_charge):
    levels = jnp.arange(1, 5, dtype=jnp.int32)
    chosen = (bead_label[None] == levels[:, None, None, None]).astype(jnp.float32)
    return jnp.sum(chosen * bead_charge[:, None, None, None], axis=0)


def macroscopic(populations, forcing):
    weights = jnp.asarray(lattice_weights(), jnp.float32)
    carried = jnp.asarray((VELOCITIES * lattice_weights()[:, None]).T, jnp.float32)
    density = jnp.einsum("q,q...->...", weights, populations, precision=HIGHEST)
    momentum = jnp.einsum("aq,q...->a...", carried, populations, precision=HIGHEST)
    velocity = (momentum + 0.5 * forcing) / density[None]
    return density, velocity


def collide_cells(populations, density, velocity, forcing, relax):
    lattice = jnp.asarray(VELOCITIES, jnp.float32)
    along_u = jnp.einsum("qa,a...->q...", lattice, velocity, precision=HIGHEST)
    along_f = jnp.einsum("qa,a...->q...", lattice, forcing, precision=HIGHEST)
    speed_sq = jnp.sum(velocity * velocity, axis=0)
    work_done = jnp.sum(velocity * forcing, axis=0)
    balance = density[None] * (1.0 + 3.0 * along_u + 4.5 * along_u * along_u - 1.5 * speed_sq[None])
    source = 3.0 * (along_f - work_done[None]) + 9.0 * along_u * along_f
    shifted = populations - balance + 0.5 * source
    return populations + source - jnp.einsum("qp,p...->q...", relax, shifted, precision=HIGHEST)


def face_flux(here_conc, next_conc, here_pot, next_pot, here_vel, next_vel, here_open, next_open, diffusivity, bias):
    valence = jnp.asarray([1.0, -1.0], jnp.float32)[:, None, None, None]
    spread = diffusivity[:, None, None, None]
    middle = 0.5 * (here_conc + next_conc)
    drift = (next_pot - here_pot - bias)[None]
    flux = -spread * ((next_conc - here_conc) + valence * middle * drift) + 0.5 * (here_vel + next_vel)[None] * middle
    return flux * (here_open * next_open)[None]


def jacobi_global(potential, permit, source):
    numerator = source
    denominator = jnp.zeros_like(source)
    for dimension in (1, 2, 0):
        for offset in (-1, 1):
            near_pot = jnp.roll(potential, offset, dimension)
            near_eps = jnp.roll(permit, offset, dimension)
            weight = 0.5 * (permit + near_eps)
            numerator = numerator + weight * near_pot
            denominator = denominator + weight
    return numerator / denominator


def transport_global(concentrations, potential, velocity, open_cells, diffusivity):
    change = jnp.zeros_like(concentrations)
    for dimension, component, bias in ((1, 0, 0.0), (2, 1, 0.0), (0, 2, EXT_FIELD)):
        flux = face_flux(concentrations, jnp.roll(concentrations, -1, dimension + 1),
                         potential, jnp.roll(potential, -1, dimension),
                         velocity[component], jnp.roll(velocity[component], -1, dimension),
                         open_cells, jnp.roll(open_cells, -1, dimension), diffusivity, bias)
        change = change + (flux - jnp.roll(flux, 1, dimension + 1))
    return concentrations - change


def stream_global(post, previous, open_cells):
    opposite = opposites()
    rows = []
    for member in range(19):
        step_x = int(VELOCITIES[member][0])
        step_y = int(VELOCITIES[member][1])
        step_z = int(VELOCITIES[member][2])
        moved = jnp.roll(post[member], (step_z, step_x, step_y), (0, 1, 2))
        source_open = jnp.roll(open_cells, (step_z, step_x, step_y), (0, 1, 2))
        rows.append(jnp.where(source_open > 0.5, moved, post[opposite[member]]))
    return jnp.where(open_cells[None] > 0.5, jnp.stack(rows), previous)


def reference(populations, concentrations, potential, permittivity, solid, bead_label, bead_charge, rates, diffusivity):
    relax = relaxation(rates)
    open_cells = (1 - solid).astype(jnp.float32)
    bead_field = bead_density(bead_label, bead_charge)
    for repeat in range(STEPS):
        charge_field = open_cells * (concentrations[0] - concentrations[1]) + bead_field
        for sweep_count in range(SWEEPS):
            potential = jacobi_global(potential, permittivity, charge_field)
        electric = jnp.stack([
            -0.5 * (jnp.roll(potential, -1, 1) - jnp.roll(potential, 1, 1)),
            -0.5 * (jnp.roll(potential, -1, 2) - jnp.roll(potential, 1, 2)),
            -0.5 * (jnp.roll(potential, -1, 0) - jnp.roll(potential, 1, 0)) + EXT_FIELD])
        forcing = FORCE_SCALE * (charge_field * open_cells)[None] * electric
        density, velocity = macroscopic(populations, forcing)
        new_conc = transport_global(concentrations, potential, velocity, open_cells, diffusivity)
        planes = lax.map(lambda item: collide_cells(item[0], item[1], item[2], item[3], relax),
                         (jnp.moveaxis(populations, 1, 0), density, jnp.moveaxis(velocity, 1, 0), jnp.moveaxis(forcing, 1, 0)))
        post = jnp.moveaxis(planes, 0, 1)
        populations = stream_global(post, populations, open_cells)
        concentrations = new_conc
    return populations, concentrations, potential
```

```python
import functools

import jax
import jax.numpy as jnp
import numpy as np
from jax import lax
from jax.experimental import pallas as pl
from jax.experimental.pallas import tpu as pltpu
from jax.sharding import PartitionSpec as P

STEPS = 8
SWEEPS = 3
FORCE_SCALE = 0.02
EXT_FIELD = 0.05
MESH = pl.DeviceIdType.MESH

VELOCITIES = [
    (0, 0, 0), (1, 0, 0), (-1, 0, 0), (0, 1, 0), (0, -1, 0), (0, 0, 1), (0, 0, -1),
    (1, 1, 0), (-1, -1, 0), (1, -1, 0), (-1, 1, 0), (1, 0, 1), (-1, 0, -1), (1, 0, -1),
    (-1, 0, 1), (0, 1, 1), (0, -1, -1), (0, 1, -1), (0, -1, 1),
]
OPPOSITE = [0] + [q + 1 if q % 2 else q - 1 for q in range(1, 19)]
X_UP, X_DOWN = (1, 7, 9, 11, 13), (2, 8, 10, 12, 14)
Y_UP, Y_DOWN = (3, 7, 10, 15, 17), (4, 8, 9, 16, 18)
DIAGONALS = ((1, 1), (1, -1), (-1, -1), (-1, 1))
LANES = 128


def isotropic(rates):
    rows = np.array([[1.0, 1.0, 1.0], [-30.0, -11.0, 8.0], [12.0, -4.0, 1.0]])
    count = np.array([1.0, 6.0, 12.0])
    weight = np.array([1.0 / 3.0, 1.0 / 18.0, 1.0 / 36.0])
    norm = np.sum(rows * rows * count[None, :], axis=1)
    strength = (1.0, rates[0], rates[1])
    return [
        [
            sum(
                float(rows[k, i] * rows[k, j] * weight[j] / (weight[i] * norm[k])) * strength[k]
                for k in range(3)
            )
            for j in range(3)
        ]
        for i in range(3)
    ]


def kernel(
    nx, ny, tx,
    rates_ref, diff_ref, bead_ref,
    pop_in, conc_in, pot_in, eps_in, solid_in, label_in,
    f_ref, conc_out, pot_out,
    post, pot, cc, velx, vely, velz, charge, scaled, wts, inv, bead, open_x, eps_x,
    face_x, face_y, face_z, face_left, bits,
    xs, xr, ys, yr, dr, pys, pyr,
    xs_sem, xr_sem, ys_sem, yr_sem, ds_sem, dr_sem,
    pxs_sem, pxr_sem, pys_sem, pyr_sem,
):
    mx, my = lax.axis_index("gx"), lax.axis_index("gy")
    up_x, down_x = lax.rem(mx + 1, nx), lax.rem(mx + nx - 1, nx)
    up_y, down_y = lax.rem(my + 1, ny), lax.rem(my + ny - 1, ny)
    to_x = ((up_x, my), (down_x, my))
    to_y = ((mx, up_y), (mx, down_y))
    to_diag = tuple(
        (up_x if dx > 0 else down_x, up_y if dy > 0 else down_y) for dx, dy in DIAGONALS
    )
    lane = lax.broadcasted_iota(jnp.int32, (8, LANES), 1)
    first, last = lane == 0, lane == LANES - 1

    barrier = pltpu.get_barrier_semaphore()
    for target in to_x + to_y + to_diag:
        pl.semaphore_signal(barrier, inc=1, device_id=target, device_id_type=MESH)
    pl.semaphore_wait(barrier, 8)

    def loop(body, carry, unroll):
        def outer(i, carry):
            for u in range(unroll):
                carry = body(i * unroll + u, carry)
            return carry

        return lax.fori_loop(0, tx // unroll, outer, carry)

    def roll(value, shift, axis):
        return pltpu.roll(value, shift, axis)

    def z_next(value):
        return roll(value, 7, 0)

    def z_prev(value):
        return roll(value, 1, 0)

    def y_prev(value, row, packed):
        return jnp.where(
            first, roll(packed, lax.rem(LANES - row, LANES), 1), roll(value, 1, 1)
        )

    def y_next(value, row, packed):
        return jnp.where(last, roll(packed, LANES - 1 - row, 1), roll(value, LANES - 1, 1))

    def pack_high(total, value, row):
        return jnp.where(lane == row, roll(value, row + 1, 1), total)

    def pack_low(total, value, row):
        return jnp.where(lane == row, roll(value, row, 1), total)

    def remote(source, target, send, receive, device):
        return pltpu.make_async_remote_copy(
            src_ref=source, dst_ref=target, send_sem=send, recv_sem=receive,
            device_id=device, device_id_type=MESH,
        )

    def x_copies(par):
        made = [
            remote(xs.at[d], xr.at[par, d], xs_sem.at[d], xr_sem.at[par, d], to_x[d])
            for d in range(2)
        ]
        for k, (dx, dy) in enumerate(DIAGONALS):
            source = xs.at[0 if dx > 0 else 1, 1 if dx == dy else 2]
            made.append(
                remote(source, dr.at[par, k], ds_sem.at[k], dr_sem.at[par, k], to_diag[k])
            )
        return made

    def y_copies(par):
        return [
            remote(ys.at[d], yr.at[par, d], ys_sem.at[d], yr_sem.at[par, d], to_y[d])
            for d in range(2)
        ]

    def pot_copies(b):
        made = [
            remote(pot.at[b, tx], pot.at[b, 0], pxs_sem.at[0], pxr_sem.at[b, 0], to_x[0]),
            remote(pot.at[b, 1], pot.at[b, tx + 1], pxs_sem.at[1], pxr_sem.at[b, 1], to_x[1]),
        ]
        for d in range(2):
            made.append(
                remote(pys.at[d], pyr.at[b, d], pys_sem.at[d], pyr_sem.at[b, d], to_y[d])
            )
        return made

    def with_corner(packed, par, k):
        dx, dy = DIAGONALS[k]
        spot = LANES - 1 if dx > 0 else tx
        shift = (spot - (LANES - 1 if dy > 0 else 0)) % LANES
        corner = dr[par, k]
        if shift:
            corner = roll(corner, shift, 1)
        return jnp.where(lane == spot, corner, packed)

    zero = jnp.zeros((8, LANES), jnp.float32)

    def begin(x, carry):
        acc = list(carry)
        opened = (1 - solid_in[x]).astype(jnp.float32)
        open_x[x + 1] = opened
        eps = eps_in[x]
        eps_x[x + 1] = eps
        start = pot_in[x]
        pot[0, x + 1] = start
        label = label_in[x]
        field = zero
        for level in range(4):
            field = jnp.where(label == level + 1, bead_ref[level], field)
        bead[x] = field
        cation, anion = conc_in[0, x], conc_in[1, x]
        cc[0, x + 1] = cation
        cc[1, x + 1] = anion
        charge[x] = opened * (cation - anion) + field
        for q in range(19):
            f_ref[q, x] = pop_in[q, x]
        for k, value in enumerate((opened, eps, start)):
            acc[k] = pack_high(acc[k], value, x)
            acc[3 + k] = pack_low(acc[3 + k], value, x)
        return tuple(acc)

    acc = loop(begin, (zero,) * 6, 1)
    for d in range(2):
        row = tx if d == 0 else 1
        for k in range(3):
            xs[d, k] = open_x[row]
            ys[d, k] = acc[3 * d + k]
        xs[d, 3] = eps_x[row]
        xs[d, 4] = pot[0, row]
        for k in range(5, 8):
            xs[d, k] = zero
        for k in range(3, 8):
            ys[d, k] = zero
        pys[d] = acc[3 * d + 2]
    moving = x_copies(1) + y_copies(1)
    for copy in moving:
        copy.start()
    for copy in moving:
        copy.wait()
    for d in range(2):
        row = 0 if d == 0 else tx + 1
        open_x[row] = xr[1, d, 0]
        eps_x[row] = xr[1, d, 3]
        pot[0, row] = xr[1, d, 4]
        pyr[0, d] = yr[1, d, 2]
    open_low = with_corner(with_corner(yr[1, 0, 0], 1, 0), 1, 3)
    open_high = with_corner(with_corner(yr[1, 1, 0], 1, 1), 1, 2)
    eps_low, eps_high = yr[1, 0, 1], yr[1, 1, 1]
    face_left[...] = yr[1, 0, 0] * ys[1, 0]
    face_x[0] = open_x[0] * open_x[1]

    def prepare(x, carry):
        eps, opened = eps_x[x + 1], open_x[x + 1]
        near = (
            eps_x[x + 2], eps_x[x],
            y_next(eps, x, eps_high), y_prev(eps, x, eps_low),
            z_next(eps), z_prev(eps),
        )
        near = [0.5 * (eps + other) for other in near]
        total = near[0] + near[1] + near[2] + near[3] + near[4] + near[5]
        whole = 1.0 / total
        inv[x] = whole
        for k in range(6):
            wts[k, x] = near[k] * whole
        scaled[x] = charge[x] * whole
        face_x[x + 1] = opened * open_x[x + 2]
        face_y[x] = opened * y_next(opened, x, open_high)
        face_z[x] = opened * z_next(opened)
        found = jnp.zeros((8, LANES), jnp.int32)
        for q in range(1, 19):
            sx, sy, sz = VELOCITIES[q]
            source = open_x[x - sx + 1]
            if sy > 0:
                source = y_prev(source, x - sx, open_low)
            elif sy < 0:
                source = y_next(source, x - sx, open_high)
            if sz:
                source = roll(source, sz % 8, 0)
            found = found + jnp.where(source > 0.5, 1 << q, 0)
        bits[x] = jnp.where(opened > 0.5, found, 0)
        return carry

    loop(prepare, 0, 1)

    rates = [rates_ref[k] for k in range(5)]
    iso = isotropic(rates)
    shear, ghost, heat, third = rates[3], rates[1], rates[2], rates[4]

    def deviator(n_shear, n_ghost):
        a, b = shear * (1.0 / n_shear), ghost * (1.0 / n_ghost)
        return (a + 4.0 * b, 0.5 * a - b, 2.0 * a - 4.0 * b, a + b)

    dev_x, dev_w = deviator(36.0, 72.0), deviator(12.0, 24.0)
    shear_off = 0.25 * shear
    odd = (0.1 + 0.4 * heat, 0.05 - 0.05 * heat, 0.2 - 0.2 * heat, 0.1 + 0.025 * heat)
    third_off = 0.125 * third
    spread = (diff_ref[0], diff_ref[1])

    def sweep(n):
        old, new = lax.rem(n, 2), lax.rem(n + 1, 2)
        low, high = pyr[old, 0], pyr[old, 1]

        def body(x, carry):
            here = pot[old, x + 1]
            value = scaled[x] + wts[0, x] * pot[old, x + 2] + wts[1, x] * pot[old, x]
            value = value + wts[2, x] * y_next(here, x, high) + wts[3, x] * y_prev(here, x, low)
            value = value + (wts[4, x] * z_next(here) + wts[5, x] * z_prev(here))
            pot[new, x + 1] = value
            return pack_high(carry[0], value, x), pack_low(carry[1], value, x)

        ends = loop(body, (zero, zero), 8)
        pys[0] = ends[0]
        pys[1] = ends[1]
        moving = pot_copies(new)
        for copy in moving:
            copy.start()
        for copy in moving:
            copy.wait()

    def collide(b):
        low, high = pyr[b, 0], pyr[b, 1]

        def body(x, carry):
            f = [f_ref[q, x] for q in range(19)]
            opened = open_x[x + 1]
            here = pot[b, x + 1]
            strength = (-0.5 * FORCE_SCALE) * (charge[x] * opened)
            fx = strength * (pot[b, x + 2] - pot[b, x])
            fy = strength * (y_next(here, x, high) - y_prev(here, x, low))
            fz = strength * (z_next(here) - z_prev(here) - 2.0 * EXT_FIELD)
            s = {q: f[q] + f[q + 1] for q in range(1, 19, 2)}
            d = {q: f[q] - f[q + 1] for q in range(1, 19, 2)}
            axis_sum = s[1] + s[3] + s[5]
            diag_sum = (s[7] + s[9]) + (s[11] + s[13]) + (s[15] + s[17])
            rho = (1.0 / 3.0) * f[0] + (1.0 / 18.0) * axis_sum + (1.0 / 36.0) * diag_sum
            hx, kx = d[7] + d[9], d[11] + d[13]
            hy, ky = d[7] - d[9], d[15] + d[17]
            hz, kz = d[11] - d[13], d[15] - d[17]
            momx = (1.0 / 18.0) * d[1] + (1.0 / 36.0) * (hx + kx) + 0.5 * fx
            momy = (1.0 / 18.0) * d[3] + (1.0 / 36.0) * (hy + ky) + 0.5 * fy
            momz = (1.0 / 18.0) * d[5] + (1.0 / 36.0) * (hz + kz) + 0.5 * fz
            over = 1.0 / rho
            ux, uy, uz = momx * over, momy * over, momz * over
            velx[x + 1] = ux
            vely[x] = uy
            velz[x] = uz
            work = ux * fx + uy * fy + uz * fz
            s0 = -3.0 * work
            k0 = s0 - 2.0 * rho + 3.0 * (momx * ux + momy * uy + momz * uz)
            wx, wy, wz = 9.0 * (fx - momx), 9.0 * (fy - momy), 9.0 * (fz - momz)
            gx, gy, gz = 3.0 * fx - 6.0 * momx, 3.0 * fy - 6.0 * momy, 3.0 * fz - 6.0 * momz
            nfx, nfy, nfz = 9.0 * fx, 9.0 * fy, 9.0 * fz

            def along(a, b, c):
                return {1: a, 3: b, 5: c, 7: a + b, 9: a - b, 11: a + c, 13: a - c, 15: b + c, 17: b - c}

            cu, cw, cf = along(ux, uy, uz), along(wx, wy, wz), along(nfx, nfy, nfz)
            xsum = {q: s[q] + k0 + cu[q] * cw[q] for q in s}
            src = {q: s0 + cu[q] * cf[q] for q in s}
            x0 = f[0] + 0.5 * k0
            bxy, cxy = xsum[7] + xsum[9], xsum[7] - xsum[9]
            bxz, cxz = xsum[11] + xsum[13], xsum[11] - xsum[13]
            byz, cyz = xsum[15] + xsum[17], xsum[15] - xsum[17]
            a_all = xsum[1] + xsum[3] + xsum[5]
            b_all = bxy + bxz + byz
            t0, t1, t2 = [r[0] * x0 + r[1] * a_all + r[2] * b_all for r in iso]
            p1, q1 = 3.0 * xsum[1] - a_all, b_all - 3.0 * byz
            p2, q2 = xsum[3] - xsum[5], bxy - bxz
            u1, u2 = dev_x[0] * p1 + dev_x[1] * q1, dev_x[2] * p1 + dev_x[3] * q1
            v1, v2 = dev_w[0] * p2 + dev_w[1] * q2, dev_w[2] * p2 + dev_w[3] * q2
            low1, low2 = t1 - u1, t2 + u2
            exy, exz, eyz = low2 + v2, low2 - v2, t2 - 2.0 * u2
            gxy, gxz, gyz = shear_off * cxy, shear_off * cxz, shear_off * cyz
            even = {
                1: t1 + 2.0 * u1, 3: low1 + v1, 5: low1 - v1,
                7: exy + gxy, 9: exy - gxy, 11: exz + gxz, 13: exz - gxz,
                15: eyz + gyz, 17: eyz - gyz,
            }

            def odd_part(d1, h, k, g, force):
                d1 = d1 + g
                both = h + k + 4.0 * g
                edge = 3.0 * force
                shared = edge - (odd[2] * d1 + odd[3] * both)
                turn = third_off * (h - k)
                return edge - (odd[0] * d1 + odd[1] * both), shared - turn, shared + turn

            ox, px, nxx = odd_part(d[1], hx, kx, gx, fx)
            oy, py, nyy = odd_part(d[3], hy, ky, gy, fy)
            oz, pz, nzz = odd_part(d[5], hz, kz, gz, fz)
            odds = {
                1: ox, 3: oy, 5: oz, 7: px + py, 9: px - py,
                11: nxx + pz, 13: nxx - pz, 15: nyy + nzz, 17: nyy - nzz,
            }
            is_open = opened > 0.5
            post[0, x + 1] = jnp.where(is_open, f[0] + s0 - t0, f[0])
            for q in range(1, 19, 2):
                ev = src[q] - even[q]
                post[q, x + 1] = jnp.where(is_open, f[q] + (ev + odds[q]), f[q + 1])
                post[q + 1, x + 1] = jnp.where(is_open, f[q + 1] + (ev - odds[q]), f[q])
            return carry

        loop(body, 0, 1)

    def pack_edges(x, carry):
        acc = list(carry)
        ions = (cc[0, x + 1], cc[1, x + 1], vely[x])
        for k in range(8):
            acc[k] = pack_high(acc[k], ions[k - 5] if k > 4 else post[Y_UP[k], x + 1], x)
        for k in range(8):
            acc[8 + k] = pack_low(acc[8 + k], ions[k - 5] if k > 4 else post[Y_DOWN[k], x + 1], x)
        return tuple(acc)

    def face_flux(a, b, vbar, drift, face, species):
        middle = 0.5 * (a + b)
        flow = middle * drift
        slope = b - a
        slope = slope + flow if species == 0 else slope - flow
        return (vbar * middle - spread[species] * slope) * face

    def transport(par, b):
        ends = [
            face_flux(
                yr[par, 0, 5 + k], ys[1, 5 + k], 0.5 * (yr[par, 0, 7] + ys[1, 7]),
                pys[1] - pyr[b, 0], face_left[...], k,
            )
            for k in range(2)
        ]
        pot_high, vel_high = pyr[b, 1], yr[par, 1, 7]
        conc_high = (yr[par, 1, 5], yr[par, 1, 6])
        below = tuple(
            face_flux(
                cc[k, 0], cc[k, 1], 0.5 * (velx[0] + velx[1]),
                pot[b, 1] - pot[b, 0], face_x[0], k,
            )
            for k in range(2)
        )

        def body(x, below):
            here = pot[b, x + 1]
            drift_x = pot[b, x + 2] - here
            drift_y = y_next(here, x, pot_high) - here
            drift_z = z_next(here) - here - EXT_FIELD
            vy, vz = vely[x], velz[x]
            vbar_x = 0.5 * (velx[x + 1] + velx[x + 2])
            vbar_y = 0.5 * (vy + y_next(vy, x, vel_high))
            vbar_z = 0.5 * (vz + z_next(vz))
            above, fresh = [], []
            for k in range(2):
                c = cc[k, x + 1]
                up = face_flux(c, cc[k, x + 2], vbar_x, drift_x, face_x[x + 1], k)
                side = face_flux(c, y_next(c, x, conc_high[k]), vbar_y, drift_y, face_y[x], k)
                deep = face_flux(c, z_next(c), vbar_z, drift_z, face_z[x], k)
                change = (up - below[k]) + (side - y_prev(side, x, ends[k])) + (deep - z_prev(deep))
                above.append(up)
                fresh.append(c - change)
            cc[0, x + 1] = fresh[0]
            cc[1, x + 1] = fresh[1]
            total = open_x[x + 1] * (fresh[0] - fresh[1]) + bead[x]
            charge[x] = total
            scaled[x] = total * inv[x]
            return tuple(above)

        loop(body, below, 2)

    def stream(par):
        low = {q: yr[par, 0, k] for k, q in enumerate(Y_UP)}
        high = {q: yr[par, 1, k] for k, q in enumerate(Y_DOWN)}
        low[7] = with_corner(low[7], par, 0)
        high[9] = with_corner(high[9], par, 1)
        high[8] = with_corner(high[8], par, 2)
        low[10] = with_corner(low[10], par, 3)

        def body(x, carry):
            mask = bits[x]
            f_ref[0, x] = post[0, x + 1]
            for q in range(1, 19):
                sx, sy, sz = VELOCITIES[q]
                value = post[q, x - sx + 1]
                if sy > 0:
                    value = y_prev(value, x - sx, low[q])
                elif sy < 0:
                    value = y_next(value, x - sx, high[q])
                if sz:
                    value = roll(value, sz % 8, 0)
                f_ref[q, x] = jnp.where((mask & (1 << q)) != 0, value, post[OPPOSITE[q], x + 1])
            return carry

        loop(body, 0, 1)

    def step(t, carry):
        par = lax.rem(t, 2)

        def one(k, carry):
            sweep(t * SWEEPS + k)
            return carry

        lax.fori_loop(0, SWEEPS, one, 0)
        b = lax.rem((t + 1) * SWEEPS, 2)
        collide(b)
        for d in range(2):
            row = tx if d == 0 else 1
            for k, q in enumerate((X_UP, X_DOWN)[d]):
                xs[d, k] = post[q, row]
            xs[d, 5] = cc[0, row]
            xs[d, 6] = cc[1, row]
            xs[d, 7] = velx[row]
        across = x_copies(par)
        for copy in across:
            copy.start()
        acc = loop(pack_edges, (zero,) * 16, 2)
        for d in range(2):
            for k in range(8):
                ys[d, k] = acc[8 * d + k]
        sideways = y_copies(par)
        for copy in sideways:
            copy.start()
        for copy in across + sideways:
            copy.wait()
        for d in range(2):
            row = 0 if d == 0 else tx + 1
            for k, q in enumerate((X_UP, X_DOWN)[d]):
                post[q, row] = xr[par, d, k]
            cc[0, row] = xr[par, d, 5]
            cc[1, row] = xr[par, d, 6]
            velx[row] = xr[par, d, 7]
        transport(par, b)
        stream(par)
        return carry

    lax.fori_loop(0, STEPS, step, 0)

    def finish(x, carry):
        conc_out[0, x] = cc[0, x + 1]
        conc_out[1, x] = cc[1, x + 1]
        pot_out[x] = pot[(STEPS * SWEEPS) % 2, x + 1]
        return carry

    loop(finish, 0, 1)


def local(nx, ny, populations, concentrations, potential, permittivity, solid, bead_label,
          bead_charge, rates, diffusivity):
    tx = populations.shape[2]

    def turn(array):
        return jnp.swapaxes(array, -3, -2)

    f32 = jnp.float32
    tile = (8, LANES)

    def vmem(*lead):
        return pltpu.VMEM(lead + tile, f32)

    dma = pltpu.SemaphoreType.DMA
    smem = pl.BlockSpec(memory_space=pltpu.SMEM)
    block = pl.BlockSpec(memory_space=pltpu.VMEM)
    outs = pl.pallas_call(
        functools.partial(kernel, nx, ny, tx),
        out_shape=[
            jax.ShapeDtypeStruct((19, tx) + tile, f32),
            jax.ShapeDtypeStruct((2, tx) + tile, f32),
            jax.ShapeDtypeStruct((tx,) + tile, f32),
        ],
        in_specs=[smem] * 3 + [block] * 6,
        out_specs=[block] * 3,
        scratch_shapes=[
            vmem(19, tx + 2), vmem(2, tx + 2), vmem(2, tx + 2), vmem(tx + 2), vmem(tx), vmem(tx),
            vmem(tx), vmem(tx), vmem(6, tx), vmem(tx), vmem(tx), vmem(tx + 2), vmem(tx + 2),
            vmem(tx + 1), vmem(tx), vmem(tx), vmem(), pltpu.VMEM((tx,) + tile, jnp.int32),
            vmem(2, 8), vmem(2, 2, 8), vmem(2, 8), vmem(2, 2, 8), vmem(2, 4), vmem(2), vmem(2, 2),
            dma((2,)), dma((2, 2)), dma((2,)), dma((2, 2)), dma((4,)), dma((2, 4)),
            dma((2,)), dma((2, 2)), dma((2,)), dma((2, 2)),
        ],
        compiler_params=pltpu.CompilerParams(
            collective_id=0, has_side_effects=True, vmem_limit_bytes=48 * 1024 * 1024
        ),
    )(
        rates, diffusivity, bead_charge,
        turn(populations), turn(concentrations), turn(potential), turn(permittivity),
        turn(solid), turn(bead_label),
    )
    return tuple(turn(array) for array in outs)


def solution(mesh):
    in_specs = (
        P(None, None, "gx", "gy"),
        P(None, None, "gx", "gy"),
        P(None, "gx", "gy"),
        P(None, "gx", "gy"),
        P(None, "gx", "gy"),
        P(None, "gx", "gy"),
        P(),
        P(),
        P(),
    )
    out_specs = (P(None, None, "gx", "gy"), P(None, None, "gx", "gy"), P(None, "gx", "gy"))
    return jax.shard_map(
        functools.partial(local, mesh.shape["gx"], mesh.shape["gy"]),
        mesh=mesh, in_specs=in_specs, out_specs=out_specs, check_vma=False,
    )
```

```python
import functools

import jax
import jax.numpy as jnp
import numpy as np
from jax import lax
from jax.experimental import pallas as pl
from jax.experimental.pallas import tpu as pltpu
from jax.sharding import PartitionSpec as P

STEPS = 8
SWEEPS = 3
FORCE_SCALE = 0.02
EXT_FIELD = 0.05
MESH = pl.DeviceIdType.MESH

VELOCITIES = [
    (0, 0, 0), (1, 0, 0), (-1, 0, 0), (0, 1, 0), (0, -1, 0), (0, 0, 1), (0, 0, -1),
    (1, 1, 0), (-1, -1, 0), (1, -1, 0), (-1, 1, 0), (1, 0, 1), (-1, 0, -1), (1, 0, -1),
    (-1, 0, 1), (0, 1, 1), (0, -1, -1), (0, 1, -1), (0, -1, 1),
]
OPPOSITE = [0] + [q + 1 if q % 2 else q - 1 for q in range(1, 19)]
X_UP, X_DOWN = (1, 7, 9, 11, 13), (2, 8, 10, 12, 14)
Y_UP, Y_DOWN = (3, 7, 10, 15, 17), (4, 8, 9, 16, 18)
DIAGONALS = ((1, 1), (1, -1), (-1, -1), (-1, 1))
LANES = 128


def isotropic(rates):
    rows = np.array([[1.0, 1.0, 1.0], [-30.0, -11.0, 8.0], [12.0, -4.0, 1.0]])
    count = np.array([1.0, 6.0, 12.0])
    weight = np.array([1.0 / 3.0, 1.0 / 18.0, 1.0 / 36.0])
    norm = np.sum(rows * rows * count[None, :], axis=1)
    strength = (1.0, rates[0], rates[1])
    return [
        [
            sum(
                float(rows[k, i] * rows[k, j] * weight[j] / (weight[i] * norm[k])) * strength[k]
                for k in range(3)
            )
            for j in range(3)
        ]
        for i in range(3)
    ]


def kernel(
    nx, ny, tx,
    rates_ref, diff_ref, bead_ref,
    pop_in, conc_in, pot_in, eps_in, solid_in, label_in,
    f_ref, conc_out, pot_out,
    post, pot, cc, velx, vely, velz, charge, scaled, wts, inv, bead, open_x, eps_x,
    face_x, face_y, face_z, face_left, bits,
    xs, xr, ys, yr, dr, pys, pyr,
    xs_sem, xr_sem, ys_sem, yr_sem, ds_sem, dr_sem,
    pxs_sem, pxr_sem, pys_sem, pyr_sem,
):
    mx, my = lax.axis_index("gx"), lax.axis_index("gy")
    up_x, down_x = lax.rem(mx + 1, nx), lax.rem(mx + nx - 1, nx)
    up_y, down_y = lax.rem(my + 1, ny), lax.rem(my + ny - 1, ny)
    to_x = ((up_x, my), (down_x, my))
    to_y = ((mx, up_y), (mx, down_y))
    to_diag = tuple(
        (up_x if dx > 0 else down_x, up_y if dy > 0 else down_y) for dx, dy in DIAGONALS
    )
    lane = lax.broadcasted_iota(jnp.int32, (8, LANES), 1)
    first, last = lane == 0, lane == LANES - 1

    barrier = pltpu.get_barrier_semaphore()
    for target in to_x + to_y + to_diag:
        pl.semaphore_signal(barrier, inc=1, device_id=target, device_id_type=MESH)
    pl.semaphore_wait(barrier, 8)

    def loop(body, carry, unroll):
        def outer(i, carry):
            for u in range(unroll):
                carry = body(i * unroll + u, carry)
            return carry

        return lax.fori_loop(0, tx // unroll, outer, carry)

    def roll(value, shift, axis):
        return pltpu.roll(value, shift, axis)

    def z_next(value):
        return roll(value, 7, 0)

    def z_prev(value):
        return roll(value, 1, 0)

    def y_prev(value, row, packed):
        return jnp.where(
            first, roll(packed, lax.rem(LANES - row, LANES), 1), roll(value, 1, 1)
        )

    def y_next(value, row, packed):
        return jnp.where(last, roll(packed, LANES - 1 - row, 1), roll(value, LANES - 1, 1))

    def pack_high(total, value, row):
        return jnp.where(lane == row, roll(value, row + 1, 1), total)

    def pack_low(total, value, row):
        return jnp.where(lane == row, roll(value, row, 1), total)

    def remote(source, target, send, receive, device):
        return pltpu.make_async_remote_copy(
            src_ref=source, dst_ref=target, send_sem=send, recv_sem=receive,
            device_id=device, device_id_type=MESH,
        )

    def x_copies(par):
        made = [
            remote(xs.at[d], xr.at[par, d], xs_sem.at[d], xr_sem.at[par, d], to_x[d])
            for d in range(2)
        ]
        for k, (dx, dy) in enumerate(DIAGONALS):
            source = xs.at[0 if dx > 0 else 1, 1 if dx == dy else 2]
            made.append(
                remote(source, dr.at[par, k], ds_sem.at[k], dr_sem.at[par, k], to_diag[k])
            )
        return made

    def y_copies(par):
        return [
            remote(ys.at[d], yr.at[par, d], ys_sem.at[d], yr_sem.at[par, d], to_y[d])
            for d in range(2)
        ]

    def pot_copies(b):
        made = [
            remote(pot.at[b, tx], pot.at[b, 0], pxs_sem.at[0], pxr_sem.at[b, 0], to_x[0]),
            remote(pot.at[b, 1], pot.at[b, tx + 1], pxs_sem.at[1], pxr_sem.at[b, 1], to_x[1]),
        ]
        for d in range(2):
            made.append(
                remote(pys.at[d], pyr.at[b, d], pys_sem.at[d], pyr_sem.at[b, d], to_y[d])
            )
        return made

    def with_corner(packed, par, k):
        dx, dy = DIAGONALS[k]
        spot = LANES - 1 if dx > 0 else tx
        shift = (spot - (LANES - 1 if dy > 0 else 0)) % LANES
        corner = dr[par, k]
        if shift:
            corner = roll(corner, shift, 1)
        return jnp.where(lane == spot, corner, packed)

    zero = jnp.zeros((8, LANES), jnp.float32)

    def begin(x, carry):
        acc = list(carry)
        opened = (1 - solid_in[x]).astype(jnp.float32)
        open_x[x + 1] = opened
        eps = eps_in[x]
        eps_x[x + 1] = eps
        start = pot_in[x]
        pot[0, x + 1] = start
        label = label_in[x]
        field = zero
        for level in range(4):
            field = jnp.where(label == level + 1, bead_ref[level], field)
        bead[x] = field
        cation, anion = conc_in[0, x], conc_in[1, x]
        cc[0, x + 1] = cation
        cc[1, x + 1] = anion
        charge[x] = opened * (cation - anion) + field
        for q in range(19):
            post[OPPOSITE[q], x + 1] = pop_in[q, x]
        for k, value in enumerate((opened, eps, start)):
            acc[k] = pack_high(acc[k], value, x)
            acc[3 + k] = pack_low(acc[3 + k], value, x)
        return tuple(acc)

    acc = loop(begin, (zero,) * 6, 1)
    for d in range(2):
        row = tx if d == 0 else 1
        for k in range(3):
            xs[d, k] = open_x[row]
            ys[d, k] = acc[3 * d + k]
        xs[d, 3] = eps_x[row]
        xs[d, 4] = pot[0, row]
        for k in range(5, 8):
            xs[d, k] = zero
        for k in range(3, 8):
            ys[d, k] = zero
        pys[d] = acc[3 * d + 2]
        for q in range(19):
            post[q, 0 if d == 0 else tx + 1] = zero
    moving = x_copies(1) + y_copies(1)
    for copy in moving:
        copy.start()
    for copy in moving:
        copy.wait()
    for d in range(2):
        row = 0 if d == 0 else tx + 1
        open_x[row] = xr[1, d, 0]
        eps_x[row] = xr[1, d, 3]
        pot[0, row] = xr[1, d, 4]
        pyr[0, d] = yr[1, d, 2]
    open_low = with_corner(with_corner(yr[1, 0, 0], 1, 0), 1, 3)
    open_high = with_corner(with_corner(yr[1, 1, 0], 1, 1), 1, 2)
    eps_low, eps_high = yr[1, 0, 1], yr[1, 1, 1]
    face_left[...] = yr[1, 0, 0] * ys[1, 0]
    face_x[0] = open_x[0] * open_x[1]

    def prepare(x, carry):
        eps, opened = eps_x[x + 1], open_x[x + 1]
        near = (
            eps_x[x + 2], eps_x[x],
            y_next(eps, x, eps_high), y_prev(eps, x, eps_low),
            z_next(eps), z_prev(eps),
        )
        near = [0.5 * (eps + other) for other in near]
        total = near[0] + near[1] + near[2] + near[3] + near[4] + near[5]
        whole = 1.0 / total
        inv[x] = whole
        for k in range(6):
            wts[k, x] = near[k] * whole
        scaled[x] = charge[x] * whole
        face_x[x + 1] = opened * open_x[x + 2]
        face_y[x] = opened * y_next(opened, x, open_high)
        face_z[x] = opened * z_next(opened)
        found = jnp.zeros((8, LANES), jnp.int32)
        for q in range(1, 19):
            sx, sy, sz = VELOCITIES[q]
            source = open_x[x - sx + 1]
            if sy > 0:
                source = y_prev(source, x - sx, open_low)
            elif sy < 0:
                source = y_next(source, x - sx, open_high)
            if sz:
                source = roll(source, sz % 8, 0)
            found = found + jnp.where(source > 0.5, 1 << q, 0)
        bits[x] = jnp.where(opened > 0.5, found, 0)
        return carry

    loop(prepare, 0, 1)

    rates = [rates_ref[k] for k in range(5)]
    iso = isotropic(rates)
    shear, ghost, heat, third = rates[3], rates[1], rates[2], rates[4]

    def deviator(n_shear, n_ghost):
        a, b = shear * (1.0 / n_shear), ghost * (1.0 / n_ghost)
        return (a + 4.0 * b, 0.5 * a - b, 2.0 * a - 4.0 * b, a + b)

    dev_x, dev_w = deviator(36.0, 72.0), deviator(12.0, 24.0)
    shear_off = 0.25 * shear
    odd = (0.1 + 0.4 * heat, 0.05 - 0.05 * heat, 0.2 - 0.2 * heat, 0.1 + 0.025 * heat)
    third_off = 0.125 * third
    spread = (diff_ref[0], diff_ref[1])

    def sweep(n, meanwhile):
        old, new = lax.rem(n, 2), lax.rem(n + 1, 2)
        low, high = pyr[old, 0], pyr[old, 1]

        def body(x, carry):
            here = pot[old, x + 1]
            value = scaled[x] + wts[0, x] * pot[old, x + 2] + wts[1, x] * pot[old, x]
            value = value + wts[2, x] * y_next(here, x, high) + wts[3, x] * y_prev(here, x, low)
            value = value + (wts[4, x] * z_next(here) + wts[5, x] * z_prev(here))
            pot[new, x + 1] = value
            return pack_high(carry[0], value, x), pack_low(carry[1], value, x)

        ends = loop(body, (zero, zero), 16)
        pys[0] = ends[0]
        pys[1] = ends[1]
        moving = pot_copies(new)
        for copy in moving:
            copy.start()
        meanwhile()
        for copy in moving:
            copy.wait()

    def collide(b):
        low, high = pyr[b, 0], pyr[b, 1]

        def body(x, carry):
            f = [f_ref[q, x] for q in range(19)]
            opened = open_x[x + 1]
            here = pot[b, x + 1]
            strength = (-0.5 * FORCE_SCALE) * (charge[x] * opened)
            fx = strength * (pot[b, x + 2] - pot[b, x])
            fy = strength * (y_next(here, x, high) - y_prev(here, x, low))
            fz = strength * (z_next(here) - z_prev(here) - 2.0 * EXT_FIELD)
            s = {q: f[q] + f[q + 1] for q in range(1, 19, 2)}
            d = {q: f[q] - f[q + 1] for q in range(1, 19, 2)}
            axis_sum = s[1] + s[3] + s[5]
            diag_sum = (s[7] + s[9]) + (s[11] + s[13]) + (s[15] + s[17])
            rho = (1.0 / 3.0) * f[0] + (1.0 / 18.0) * axis_sum + (1.0 / 36.0) * diag_sum
            hx, kx = d[7] + d[9], d[11] + d[13]
            hy, ky = d[7] - d[9], d[15] + d[17]
            hz, kz = d[11] - d[13], d[15] - d[17]
            momx = (1.0 / 18.0) * d[1] + (1.0 / 36.0) * (hx + kx) + 0.5 * fx
            momy = (1.0 / 18.0) * d[3] + (1.0 / 36.0) * (hy + ky) + 0.5 * fy
            momz = (1.0 / 18.0) * d[5] + (1.0 / 36.0) * (hz + kz) + 0.5 * fz
            over = 1.0 / rho
            ux, uy, uz = momx * over, momy * over, momz * over
            velx[x + 1] = ux
            vely[x] = uy
            velz[x] = uz
            work = ux * fx + uy * fy + uz * fz
            s0 = -3.0 * work
            k0 = s0 - 2.0 * rho + 3.0 * (momx * ux + momy * uy + momz * uz)
            wx, wy, wz = 9.0 * (fx - momx), 9.0 * (fy - momy), 9.0 * (fz - momz)
            gx, gy, gz = 3.0 * fx - 6.0 * momx, 3.0 * fy - 6.0 * momy, 3.0 * fz - 6.0 * momz
            nfx, nfy, nfz = 9.0 * fx, 9.0 * fy, 9.0 * fz

            def along(a, b, c):
                return {1: a, 3: b, 5: c, 7: a + b, 9: a - b, 11: a + c, 13: a - c, 15: b + c, 17: b - c}

            cu, cw, cf = along(ux, uy, uz), along(wx, wy, wz), along(nfx, nfy, nfz)
            xsum = {q: s[q] + k0 + cu[q] * cw[q] for q in s}
            src = {q: s0 + cu[q] * cf[q] for q in s}
            x0 = f[0] + 0.5 * k0
            bxy, cxy = xsum[7] + xsum[9], xsum[7] - xsum[9]
            bxz, cxz = xsum[11] + xsum[13], xsum[11] - xsum[13]
            byz, cyz = xsum[15] + xsum[17], xsum[15] - xsum[17]
            a_all = xsum[1] + xsum[3] + xsum[5]
            b_all = bxy + bxz + byz
            t0, t1, t2 = [r[0] * x0 + r[1] * a_all + r[2] * b_all for r in iso]
            p1, q1 = 3.0 * xsum[1] - a_all, b_all - 3.0 * byz
            p2, q2 = xsum[3] - xsum[5], bxy - bxz
            u1, u2 = dev_x[0] * p1 + dev_x[1] * q1, dev_x[2] * p1 + dev_x[3] * q1
            v1, v2 = dev_w[0] * p2 + dev_w[1] * q2, dev_w[2] * p2 + dev_w[3] * q2
            low1, low2 = t1 - u1, t2 + u2
            exy, exz, eyz = low2 + v2, low2 - v2, t2 - 2.0 * u2
            gxy, gxz, gyz = shear_off * cxy, shear_off * cxz, shear_off * cyz
            even = {
                1: t1 + 2.0 * u1, 3: low1 + v1, 5: low1 - v1,
                7: exy + gxy, 9: exy - gxy, 11: exz + gxz, 13: exz - gxz,
                15: eyz + gyz, 17: eyz - gyz,
            }

            def odd_part(d1, h, k, g, force):
                d1 = d1 + g
                both = h + k + 4.0 * g
                edge = 3.0 * force
                shared = edge - (odd[2] * d1 + odd[3] * both)
                turn = third_off * (h - k)
                return edge - (odd[0] * d1 + odd[1] * both), shared - turn, shared + turn

            ox, px, nxx = odd_part(d[1], hx, kx, gx, fx)
            oy, py, nyy = odd_part(d[3], hy, ky, gy, fy)
            oz, pz, nzz = odd_part(d[5], hz, kz, gz, fz)
            odds = {
                1: ox, 3: oy, 5: oz, 7: px + py, 9: px - py,
                11: nxx + pz, 13: nxx - pz, 15: nyy + nzz, 17: nyy - nzz,
            }
            is_open = opened > 0.5
            post[0, x + 1] = jnp.where(is_open, f[0] + s0 - t0, f[0])
            for q in range(1, 19, 2):
                ev = src[q] - even[q]
                post[q, x + 1] = jnp.where(is_open, f[q] + (ev + odds[q]), f[q + 1])
                post[q + 1, x + 1] = jnp.where(is_open, f[q + 1] + (ev - odds[q]), f[q])
            return carry

        loop(body, 0, 2)

    def pack_edges(x, carry):
        acc = list(carry)
        ions = (cc[0, x + 1], cc[1, x + 1], vely[x])
        for k in range(8):
            acc[k] = pack_high(acc[k], ions[k - 5] if k > 4 else post[Y_UP[k], x + 1], x)
        for k in range(8):
            acc[8 + k] = pack_low(acc[8 + k], ions[k - 5] if k > 4 else post[Y_DOWN[k], x + 1], x)
        return tuple(acc)

    def face_flux(a, b, vbar, drift, face, species):
        middle = 0.5 * (a + b)
        flow = middle * drift
        slope = b - a
        slope = slope + flow if species == 0 else slope - flow
        return (vbar * middle - spread[species] * slope) * face

    def transport(par, b):
        ends = [
            face_flux(
                yr[par, 0, 5 + k], ys[1, 5 + k], 0.5 * (yr[par, 0, 7] + ys[1, 7]),
                pys[1] - pyr[b, 0], face_left[...], k,
            )
            for k in range(2)
        ]
        pot_high, vel_high = pyr[b, 1], yr[par, 1, 7]
        conc_high = (yr[par, 1, 5], yr[par, 1, 6])
        below = tuple(
            face_flux(
                cc[k, 0], cc[k, 1], 0.5 * (velx[0] + velx[1]),
                pot[b, 1] - pot[b, 0], face_x[0], k,
            )
            for k in range(2)
        )

        def body(x, below):
            here = pot[b, x + 1]
            drift_x = pot[b, x + 2] - here
            drift_y = y_next(here, x, pot_high) - here
            drift_z = z_next(here) - here - EXT_FIELD
            vy, vz = vely[x], velz[x]
            vbar_x = 0.5 * (velx[x + 1] + velx[x + 2])
            vbar_y = 0.5 * (vy + y_next(vy, x, vel_high))
            vbar_z = 0.5 * (vz + z_next(vz))
            above, fresh = [], []
            for k in range(2):
                c = cc[k, x + 1]
                up = face_flux(c, cc[k, x + 2], vbar_x, drift_x, face_x[x + 1], k)
                side = face_flux(c, y_next(c, x, conc_high[k]), vbar_y, drift_y, face_y[x], k)
                deep = face_flux(c, z_next(c), vbar_z, drift_z, face_z[x], k)
                change = (up - below[k]) + (side - y_prev(side, x, ends[k])) + (deep - z_prev(deep))
                above.append(up)
                fresh.append(c - change)
            cc[0, x + 1] = fresh[0]
            cc[1, x + 1] = fresh[1]
            total = open_x[x + 1] * (fresh[0] - fresh[1]) + bead[x]
            charge[x] = total
            scaled[x] = total * inv[x]
            return tuple(above)

        loop(body, below, 4)

    def stream(par, begun, start, stop):
        low = {q: yr[par, 0, k] for k, q in enumerate(Y_UP)}
        high = {q: yr[par, 1, k] for k, q in enumerate(Y_DOWN)}
        low[7] = with_corner(low[7], par, 0)
        high[9] = with_corner(high[9], par, 1)
        high[8] = with_corner(high[8], par, 2)
        low[10] = with_corner(low[10], par, 3)

        def body(x):
            mask = jnp.where(begun, bits[x], 0)
            f_ref[0, x] = post[0, x + 1]
            for q in range(1, 19):
                sx, sy, sz = VELOCITIES[q]
                value = post[q, x - sx + 1]
                if sy > 0:
                    value = y_prev(value, x - sx, low[q])
                elif sy < 0:
                    value = y_next(value, x - sx, high[q])
                if sz:
                    value = roll(value, sz % 8, 0)
                f_ref[q, x] = jnp.where((mask & (1 << q)) != 0, value, post[OPPOSITE[q], x + 1])

        def rows(i, carry):
            for u in range(4):
                body(i * 4 + u)
            return carry

        lax.fori_loop(start, stop, rows, 0)

    groups = tx // 4

    def step(t, carry):
        par = lax.rem(t, 2)

        def one(k, carry):
            start, stop = lax.div(k * groups, SWEEPS), lax.div((k + 1) * groups, SWEEPS)
            sweep(t * SWEEPS + k, lambda: stream(1 - par, t > 0, start, stop))
            return carry

        lax.fori_loop(0, SWEEPS, one, 0)
        b = lax.rem((t + 1) * SWEEPS, 2)
        collide(b)
        for d in range(2):
            row = tx if d == 0 else 1
            for k, q in enumerate((X_UP, X_DOWN)[d]):
                xs[d, k] = post[q, row]
            xs[d, 5] = cc[0, row]
            xs[d, 6] = cc[1, row]
            xs[d, 7] = velx[row]
        across = x_copies(par)
        for copy in across:
            copy.start()
        acc = loop(pack_edges, (zero,) * 16, 4)
        for d in range(2):
            for k in range(8):
                ys[d, k] = acc[8 * d + k]
        sideways = y_copies(par)
        for copy in sideways:
            copy.start()
        for copy in across + sideways:
            copy.wait()
        for d in range(2):
            row = 0 if d == 0 else tx + 1
            for k, q in enumerate((X_UP, X_DOWN)[d]):
                post[q, row] = xr[par, d, k]
            cc[0, row] = xr[par, d, 5]
            cc[1, row] = xr[par, d, 6]
            velx[row] = xr[par, d, 7]
        transport(par, b)
        return carry

    lax.fori_loop(0, STEPS, step, 0)
    stream((STEPS - 1) % 2, True, 0, groups)

    def finish(x, carry):
        conc_out[0, x] = cc[0, x + 1]
        conc_out[1, x] = cc[1, x + 1]
        pot_out[x] = pot[(STEPS * SWEEPS) % 2, x + 1]
        return carry

    loop(finish, 0, 1)


def local(nx, ny, populations, concentrations, potential, permittivity, solid, bead_label,
          bead_charge, rates, diffusivity):
    tx = populations.shape[2]

    def turn(array):
        return jnp.swapaxes(array, -3, -2)

    f32 = jnp.float32
    tile = (8, LANES)

    def vmem(*lead):
        return pltpu.VMEM(lead + tile, f32)

    dma = pltpu.SemaphoreType.DMA
    smem = pl.BlockSpec(memory_space=pltpu.SMEM)
    block = pl.BlockSpec(memory_space=pltpu.VMEM)
    outs = pl.pallas_call(
        functools.partial(kernel, nx, ny, tx),
        out_shape=[
            jax.ShapeDtypeStruct((19, tx) + tile, f32),
            jax.ShapeDtypeStruct((2, tx) + tile, f32),
            jax.ShapeDtypeStruct((tx,) + tile, f32),
        ],
        in_specs=[smem] * 3 + [block] * 6,
        out_specs=[block] * 3,
        scratch_shapes=[
            vmem(19, tx + 2), vmem(2, tx + 2), vmem(2, tx + 2), vmem(tx + 2), vmem(tx), vmem(tx),
            vmem(tx), vmem(tx), vmem(6, tx), vmem(tx), vmem(tx), vmem(tx + 2), vmem(tx + 2),
            vmem(tx + 1), vmem(tx), vmem(tx), vmem(), pltpu.VMEM((tx,) + tile, jnp.int32),
            vmem(2, 8), vmem(2, 2, 8), vmem(2, 8), vmem(2, 2, 8), vmem(2, 4), vmem(2), vmem(2, 2),
            dma((2,)), dma((2, 2)), dma((2,)), dma((2, 2)), dma((4,)), dma((2, 4)),
            dma((2,)), dma((2, 2)), dma((2,)), dma((2, 2)),
        ],
        compiler_params=pltpu.CompilerParams(
            collective_id=0, has_side_effects=True, vmem_limit_bytes=48 * 1024 * 1024
        ),
    )(
        rates, diffusivity, bead_charge,
        turn(populations), turn(concentrations), turn(potential), turn(permittivity),
        turn(solid), turn(bead_label),
    )
    return tuple(turn(array) for array in outs)


def solution(mesh):
    in_specs = (
        P(None, None, "gx", "gy"),
        P(None, None, "gx", "gy"),
        P(None, "gx", "gy"),
        P(None, "gx", "gy"),
        P(None, "gx", "gy"),
        P(None, "gx", "gy"),
        P(),
        P(),
        P(),
    )
    out_specs = (P(None, None, "gx", "gy"), P(None, None, "gx", "gy"), P(None, "gx", "gy"))
    return jax.shard_map(
        functools.partial(local, mesh.shape["gx"], mesh.shape["gy"]),
        mesh=mesh, in_specs=in_specs, out_specs=out_specs, check_vma=False,
    )
```
